256 devices in a mesh: lvl: 2 (over z_hi), tile: 128 (over x, z_lo, y, core).
Axes of the slice: x: 4, y: 4, z: 8 (z_hi: 2, z_lo: 4; z = z_hi * 4 + z_lo), core: 2. Of those that a mesh axis runs over, the one named last changes fastest.
Arguments:
- velocity: float32 [3, 4, 512, 512], P(None, None, 'tile'), may hold values from -3 to 3
- dumbbells: float32 [2, 3, 8, 4, 512, 512], P('lvl', None, None, None, 'tile'), may hold values from -2.97 to 2.97, as said below
- increments: bfloat16 [2, 2, 3, 8, 4, 512, 512], P('lvl', None, None, None, None, 'tile'), may hold values from -5 to 5
Outputs:
- velocity_next: float32 [3, 4, 512, 512], P(None, None, 'tile')
- stress: float32 [6, 4, 512, 512], P(None, None, 'tile')
- dumbbells_next: float32 [2, 3, 8, 4, 512, 512], P('lvl', None, None, None, 'tile')
The draws below stay inside these ranges and needn't reach their ends.
Inputs may be any that keep to these rules, and one draw needn't show every extreme that they name: `dumbbells`: every dumbbell's length is at most 2.97.
All inputs are finite; a program needn't handle non-finite values.
Results may differ from the reference program's by a relative error of at most 0.0006.
Values sent between devices are 32-bit elements; how exact they have to be, the bound alone decides.
No kernel may reach another device: no remote copies, remote signals or barrier semaphores. Data moves between devices by JAX's collectives and lax.ppermute only.
A program may use at most 64 MiB of HBM per device.

```python
import math
import jax
import jax.numpy as jnp
from jax import lax

PLANES = 4
NZ = 512
SAMP = 8
NY = 512


def draw_dumbbells(key, part):
    key = jax.random.fold_in(key, 7)
    extent = (2, 3, SAMP, PLANES, NY, NZ)
    raw = 1.3 * jax.random.normal(key, extent, jnp.float32)
    length2 = raw[:, 0] * raw[:, 0] + raw[:, 1] * raw[:, 1] + raw[:, 2] * raw[:, 2]
    factor = jnp.minimum(1.0, 2.97 / jnp.sqrt(jnp.maximum(length2, 2.97 * 2.97)))
    return raw * factor[:, None]


def levels(stream_key, shape, pieces, least, high):
    loudness = 1.0
    for position, shards_of in pieces:
        draws = jax.random.uniform(jax.random.fold_in(jax.random.fold_in(stream_key, 6), position), (shards_of,), jnp.float32, least / len(pieces), high / len(pieces))
        loudness = loudness * jnp.repeat(jnp.exp(draws), shape[position] // shards_of).reshape((-1,) + (1,) * (len(shape) - 1 - position))
    return loudness


def normal_values(rng, dims, scale, reach, cuts=(), dtype=jnp.bfloat16):
    result = jax.random.normal(rng, dims, jnp.float32) * scale
    if len(cuts) > 0:
        result = levels(rng, dims, cuts, -0.22, 0.18) * result
    return jnp.clip(result, min=-reach, max=reach).astype(dtype)


def setup_inputs(seed: int = 0) -> dict:
    key_of = jax.random.split(jax.random.key(seed), 4)
    velocity = normal_values(key_of[0], (3, PLANES, NY, NZ), 0.5, 3.0, ((2, 128),), jnp.float32)
    dumbbells = draw_dumbbells(jax.random.fold_in(key_of[3], 71), 0)
    increments = normal_values(key_of[2], (2, 2, 3, SAMP, PLANES, NY, NZ), 1.0, 5.0, ((0, 2), (5, 128)))
    return dict(velocity=velocity, dumbbells=dumbbells, increments=increments)


STEP_TIME = 0.25
WEISSENBERG = 1.0
SPRING_LIMIT = 10.0
RADIUS_CAP = 3.0
VISCOSITY = 0.5
POLYMER_WEIGHT = 0.2
NOISE_GAIN = math.sqrt(STEP_TIME / (2.0 * WEISSENBERG))
COMPONENT = ((0, 3, 4), (3, 1, 5), (4, 5, 2))

def advance(state, kappa, noise, span):
    spring = 1.0 / (1.0 - (state[0] * state[0] + state[1] * state[1] + state[2] * state[2]) / SPRING_LIMIT)
    moved = []
    for row_axis in range(3):
        stretch = kappa[row_axis, 0][None] * state[0] + kappa[row_axis, 1][None] * state[1] + kappa[row_axis, 2][None] * state[2]
        moved.append(state[row_axis] + span * (stretch - spring * state[row_axis] / (2.0 * WEISSENBERG)) + NOISE_GAIN * noise[row_axis])
    length2 = moved[0] * moved[0] + moved[1] * moved[1] + moved[2] * moved[2]
    factor = jnp.minimum(1.0, RADIUS_CAP / jnp.sqrt(jnp.maximum(length2, RADIUS_CAP * RADIUS_CAP)))
    return jnp.stack([entry * factor for entry in moved])

def kramers(state):
    spring = 1.0 / (1.0 - (state[0] * state[0] + state[1] * state[1] + state[2] * state[2]) / SPRING_LIMIT)
    return jnp.stack([state[0] * state[0] * spring, state[1] * state[1] * spring, state[2] * state[2] * spring, state[0] * state[1] * spring, state[0] * state[2] * spring, state[1] * state[2] * spring])

def coarsen(field):
    extent = field.shape
    leading = extent[:-3]
    blocked = field.reshape(leading + (extent[-3] // 2, 2, extent[-2] // 2, 2, extent[-1] // 2, 2))
    return lax.optimization_barrier(jnp.mean(blocked, axis=(-5, -3, -1)))

def spread(field):
    extent = field.shape
    leading = extent[:-3]
    widened = jnp.broadcast_to(field[..., :, None, :, None, :, None], leading + (extent[-3], 2, extent[-2], 2, extent[-1], 2))
    return widened.reshape(leading + (2 * extent[-3], 2 * extent[-2], 2 * extent[-1]))

def finish(moments):
    identity = jnp.array([1.0, 1.0, 1.0, 0.0, 0.0, 0.0], jnp.float32).reshape(6, 1, 1, 1)
    return (moments - identity) / WEISSENBERG

def wall_pair(field):
    widths = [(0, 0)] * (field.ndim - 3) + [(1, 1), (0, 0), (0, 0)]
    padded = jnp.pad(field, widths)
    return (padded[..., 2:, :, :], padded[..., :-2, :, :])

def depth_pair(field):
    return (jnp.roll(field, -1, axis=-1), jnp.roll(field, 1, axis=-1))

def row_pair(field):
    return (jnp.roll(field, -1, axis=-2), jnp.roll(field, 1, axis=-2))

def velocity_terms(velocity, pairs):
    gradient = jnp.stack([(pairs[direction][0] - pairs[direction][1]) * 0.5 for direction in range(3)], axis=1)
    laplace = pairs[0][0] + pairs[0][1] + pairs[1][0] + pairs[1][1] + pairs[2][0] + pairs[2][1] - 6.0 * velocity
    carried = velocity[0][None] * gradient[:, 0] + velocity[1][None] * gradient[:, 1] + velocity[2][None] * gradient[:, 2]
    return (gradient, laplace, carried)

def divergence(pairs):
    result_rows = []
    for row_axis in range(3):
        total_force = jnp.zeros_like(pairs[0][0][0])
        for direction in range(3):
            index_comp = COMPONENT[row_axis][direction]
            total_force = total_force + (pairs[direction][0][index_comp] - pairs[direction][1][index_comp]) * 0.5
        result_rows.append(total_force)
    return jnp.stack(result_rows)

def reference(velocity, dumbbells, increments):
    gradient, laplace, carried = velocity_terms(velocity, [wall_pair(velocity), row_pair(velocity), depth_pair(velocity)])
    kappa_coarse = spread(coarsen(gradient))
    block_rows = math.gcd(NY, 32)
    blocks_count = NY // block_rows

    def cutting(field):
        extent = field.shape
        blocked = field.reshape(extent[:-2] + (blocks_count, block_rows, extent[-1]))
        return jnp.moveaxis(blocked, -3, 0)

    def joining(field):
        moved_back = jnp.moveaxis(field, 0, -3)
        extent = moved_back.shape
        return moved_back.reshape(extent[:-3] + (extent[-3] * extent[-2], extent[-1]))
    halves = increments.astype(jnp.float32)

    def per_block(operands):
        state_zero, state_one, first_zero, second_zero, first_one, second_one, kappa_here, kappa_low = operands
        advanced = advance(state_zero, kappa_here, first_zero + second_zero, STEP_TIME)
        base = finish(lax.optimization_barrier(jnp.mean(kramers(advanced), axis=1)))
        fine_path = advance(advance(state_one, kappa_low, first_one, 0.5 * STEP_TIME), kappa_low, second_one, 0.5 * STEP_TIME)
        coarse_path = advance(state_one, kappa_low, first_one + second_one, STEP_TIME)
        correction = (coarsen(lax.optimization_barrier(jnp.mean(kramers(fine_path), axis=1))) - coarsen(lax.optimization_barrier(jnp.mean(kramers(coarse_path), axis=1)))) / WEISSENBERG
        return (advanced, fine_path, base + spread(correction))
    operands = tuple((cutting(field) for field in (dumbbells[0], dumbbells[1], halves[0, 0], halves[0, 1], halves[1, 0], halves[1, 1], gradient, kappa_coarse)))
    level_zero, level_one, stress_blocks = lax.map(per_block, operands)
    stress = joining(stress_blocks)
    dumbbells_next = jnp.stack([joining(level_zero), joining(level_one)])
    force = divergence([wall_pair(stress), row_pair(stress), depth_pair(stress)])
    velocity_next = velocity + STEP_TIME * (VISCOSITY * laplace - carried + POLYMER_WEIGHT * force)
    return (velocity_next, stress, dumbbells_next)
```

```python
import functools
import math

import jax
import jax.numpy as jnp
from jax import lax
from jax.experimental import pallas as pl
from jax.experimental.pallas import tpu as pltpu
from jax.sharding import PartitionSpec as P

STEP_TIME = 0.25
SPRING_LIMIT = 10.0
RADIUS_CAP = 3.0
VISCOSITY = 0.5
POLYMER_WEIGHT = 0.2
NOISE_GAIN = math.sqrt(STEP_TIME / 2.0)
PLANES = 4
SAMPLES = 8
PAIRS = ((0, 0), (1, 1), (2, 2), (0, 1), (0, 2), (1, 2))
RIM = (3, 1, 5)
REST = (0, 2, 4)
F32 = jnp.float32


def view(field):
    lead = field.shape[:-2]
    split = field.reshape(lead + (4, 4, 128))
    return jnp.swapaxes(split, -3, -2).reshape(lead + (16, 128))


def unview(field):
    lead = field.shape[:-2]
    split = field.reshape(lead + (4, 4, 128))
    return jnp.swapaxes(split, -3, -2).reshape(lead + (4, 512))


def row_of():
    return lax.rem(lax.broadcasted_iota(jnp.int32, (16, 128), 0), 4)


def lane_of():
    return lax.broadcasted_iota(jnp.int32, (16, 128), 1)


def column_pair(cells, lane):
    after = pltpu.roll(jnp.where(lane == 0, pltpu.roll(cells, 12, 0), cells), 127, 1)
    before = pltpu.roll(jnp.where(lane == 127, pltpu.roll(cells, 4, 0), cells), 1, 1)
    return after, before


def row_pair(cells, following, preceding, row):
    after = jnp.where(row == 3, pltpu.roll(following, 3, 0), pltpu.roll(cells, 15, 0))
    before = jnp.where(row == 0, pltpu.roll(preceding, 13, 0), pltpu.roll(cells, 1, 0))
    return after, before


def plane_pair(planes, p):
    zero = jnp.zeros_like(planes[0])
    after = planes[p + 1] if p + 1 < PLANES else zero
    before = planes[p - 1] if p > 0 else zero
    return after, before


def neighbours(core, mate, far):
    at_first = core == 0
    following = [jnp.where(at_first, m, f) for m, f in zip(mate, far)]
    preceding = [jnp.where(at_first, f, m) for m, f in zip(mate, far)]
    return following, preceding


def quad_sum(cells, row, lane):
    even_row = lax.rem(row, 2) == 0
    cells = cells + jnp.where(even_row, pltpu.roll(cells, 15, 0), pltpu.roll(cells, 1, 0))
    even_lane = lax.rem(lane, 2) == 0
    return cells + jnp.where(even_lane, pltpu.roll(cells, 127, 1), pltpu.roll(cells, 1, 1))


def spring_of(state):
    return 1.0 / (
        1.0
        - (state[0] * state[0] + state[1] * state[1] + state[2] * state[2]) * (1.0 / SPRING_LIMIT)
    )


def drift_of(state, kappa):
    half_spring = 0.5 * spring_of(state)
    return [
        kappa[a][0] * state[0] + kappa[a][1] * state[1] + kappa[a][2] * state[2]
        - half_spring * state[a]
        for a in range(3)
    ]


def capped(moved):
    length2 = moved[0] * moved[0] + moved[1] * moved[1] + moved[2] * moved[2]
    factor = jnp.minimum(1.0, RADIUS_CAP * lax.rsqrt(jnp.maximum(length2, RADIUS_CAP * RADIUS_CAP)))
    return [entry * factor for entry in moved]


def moments(state):
    spring = spring_of(state)
    scaled = [spring * state[a] for a in range(3)]
    return [scaled[a] * state[b] for a, b in PAIRS]


def advance_kernel(vel, mate, far, state, noise, moved, rim, rest):
    level = lax.axis_index("lvl")
    core = lax.rem(lax.axis_index("tile"), 2)
    row, lane = row_of(), lane_of()
    velocity = [[vel[a, p] for p in range(PLANES)] for a in range(3)]

    def gradient(p):
        result = []
        for a in range(3):
            following, preceding = neighbours(core, [mate[a, p]], [far[a, p]])
            pairs = (
                plane_pair(velocity[a], p),
                row_pair(velocity[a][p], following[0], preceding[0], row),
                column_pair(velocity[a][p], lane),
            )
            result.append([(after - before) * 0.5 for after, before in pairs])
        return result

    def emit(p, values):
        for i, c in enumerate(RIM):
            rim[i, p] = values[c]
        for i, c in enumerate(REST):
            rest[i, p] = values[c]

    @pl.when(level == 0)
    def _():
        for p in range(PLANES):
            kappa = gradient(p)

            def body(s, sums, p=p, kappa=kappa):
                q = [state[a, s, p] for a in range(3)]
                xi = [noise[0, a, s, p].astype(F32) + noise[1, a, s, p].astype(F32) for a in range(3)]
                drift = drift_of(q, kappa)
                out = capped([q[a] + STEP_TIME * drift[a] + NOISE_GAIN * xi[a] for a in range(3)])
                for a in range(3):
                    moved[a, s, p] = out[a]
                return tuple(t + m for t, m in zip(sums, moments(out)))

            sums = lax.fori_loop(0, SAMPLES, body, (jnp.zeros((16, 128), F32),) * 6, unroll=2)
            emit(p, [t * (1.0 / SAMPLES) - (1.0 if c < 3 else 0.0) for c, t in enumerate(sums)])

    @pl.when(level != 0)
    def _():
        for pair in range(PLANES // 2):
            first, second = gradient(2 * pair), gradient(2 * pair + 1)
            kappa = [
                [quad_sum(first[a][b] + second[a][b], row, lane) * 0.125 for b in range(3)]
                for a in range(3)
            ]

            def body(s, sums, pair=pair, kappa=kappa):
                for p in (2 * pair, 2 * pair + 1):
                    q = [state[a, s, p] for a in range(3)]
                    xa = [noise[0, a, s, p].astype(F32) for a in range(3)]
                    xb = [noise[1, a, s, p].astype(F32) for a in range(3)]
                    drift = drift_of(q, kappa)
                    coarse = capped(
                        [q[a] + STEP_TIME * drift[a] + NOISE_GAIN * (xa[a] + xb[a]) for a in range(3)]
                    )
                    half = capped(
                        [q[a] + (0.5 * STEP_TIME) * drift[a] + NOISE_GAIN * xa[a] for a in range(3)]
                    )
                    drift = drift_of(half, kappa)
                    fine = capped(
                        [half[a] + (0.5 * STEP_TIME) * drift[a] + NOISE_GAIN * xb[a] for a in range(3)]
                    )
                    for a in range(3):
                        moved[a, s, p] = fine[a]
                    sums = tuple(
                        t + (f - c) for t, f, c in zip(sums, moments(fine), moments(coarse))
                    )
                return sums

            sums = lax.fori_loop(0, SAMPLES, body, (jnp.zeros((16, 128), F32),) * 6)
            values = [quad_sum(t, row, lane) * (1.0 / 64.0) for t in sums]
            emit(2 * pair, values)
            emit(2 * pair + 1, values)


def join_kernel(own, other, total, toward_far, toward_mate):
    core = lax.rem(lax.axis_index("tile"), 2)
    total[...] = own[...] + other[...]
    far_row = core * 3
    for i in range(3):
        for p in range(PLANES):
            toward_far[i, p] = total[i, p, pl.ds(far_row, 4, stride=4), :]
            toward_mate[i, p] = total[i, p, pl.ds(3 - far_row, 4, stride=4), :]


def final_kernel(vel, mate, far, rim, rest, rest_other, rim_far, rim_mate, velocity_next, stress):
    core = lax.rem(lax.axis_index("tile"), 2)
    row, lane = row_of(), lane_of()
    for i, c in enumerate(RIM):
        stress[c] = rim[i]
    for i, c in enumerate(REST):
        stress[c] = rest[i] + rest_other[i]
    velocity = [[vel[a, p] for p in range(PLANES)] for a in range(3)]
    walls = [[stress[c, p] for p in range(PLANES)] for c in (0, 3, 4)]
    for p in range(PLANES):
        for a in range(3):
            following, preceding = neighbours(core, [mate[a, p]], [far[a, p]])
            own = velocity[a][p]
            pairs = (
                plane_pair(velocity[a], p),
                row_pair(own, following[0], preceding[0], row),
                column_pair(own, lane),
            )
            laplace = -6.0 * own
            carried = jnp.zeros_like(own)
            for b, (after, before) in enumerate(pairs):
                laplace = laplace + (after + before)
                carried = carried + velocity[b][p] * ((after - before) * 0.5)
            from_far = jnp.concatenate(
                [jnp.broadcast_to(rim_far[a, p, j : j + 1, :], (4, 128)) for j in range(4)], axis=0
            )
            from_mate = jnp.concatenate(
                [jnp.broadcast_to(rim_mate[a, p, j : j + 1, :], (4, 128)) for j in range(4)], axis=0
            )
            following, preceding = neighbours(core, [from_mate], [from_far])
            here = stress[RIM[a], p]
            y_after = jnp.where(row == 3, following[0], pltpu.roll(here, 15, 0))
            y_before = jnp.where(row == 0, preceding[0], pltpu.roll(here, 1, 0))
            x_after, x_before = plane_pair(walls[a], p)
            z_after, z_before = column_pair(stress[(4, 5, 2)[a], p], lane)
            force = (x_after - x_before) * 0.5 + (y_after - y_before) * 0.5 + (z_after - z_before) * 0.5
            velocity_next[a, p] = own + STEP_TIME * (
                VISCOSITY * laplace - carried + POLYMER_WEIGHT * force
            )


def shape(*extent):
    return jax.ShapeDtypeStruct(extent, F32)


def far_pairs(tiles):
    pairs = []
    for l in range(2):
        for t in range(1, tiles, 2):
            u = (t + 1) % tiles
            m = 1 - l if (t // 8) % 4 == 3 and t % 8 == 7 else l
            pairs += [(l * tiles + t, m * tiles + u), (m * tiles + u, l * tiles + t)]
    return pairs


def local(velocity, dumbbells, increments):
    tiles = lax.axis_size("tile")
    far_swap = far_pairs(tiles)
    mate_swap = [(t, t ^ 1) for t in range(tiles)]
    level_swap = [(0, 1), (1, 0)]
    vel = view(velocity)
    far = lax.ppermute(vel, ("lvl", "tile"), far_swap)
    mate = lax.ppermute(vel, "tile", mate_swap)
    moved, rim, rest = pl.pallas_call(
        advance_kernel,
        out_shape=[shape(3, SAMPLES, PLANES, 16, 128), shape(3, PLANES, 16, 128), shape(3, PLANES, 16, 128)],
    )(vel, mate, far, view(dumbbells[0]), view(increments[0]))
    rim_other = lax.ppermute(rim, "lvl", level_swap)
    rest_other = lax.ppermute(rest, "lvl", level_swap)
    rim_total, toward_far, toward_mate = pl.pallas_call(
        join_kernel,
        out_shape=[shape(3, PLANES, 16, 128), shape(3, PLANES, 4, 128), shape(3, PLANES, 4, 128)],
    )(rim, rim_other)
    rim_far = lax.ppermute(toward_far, ("lvl", "tile"), far_swap)
    rim_mate = lax.ppermute(toward_mate, "tile", mate_swap)
    velocity_next, stress = pl.pallas_call(
        final_kernel,
        out_shape=[shape(3, PLANES, 16, 128), shape(6, PLANES, 16, 128)],
    )(vel, mate, far, rim_total, rest, rest_other, rim_far, rim_mate)
    return (unview(velocity_next), unview(stress), unview(moved)[None])


def solution(mesh):
    in_specs = (
        P(None, None, "tile", None),
        P("lvl", None, None, None, "tile", None),
        P("lvl", None, None, None, None, "tile", None),
    )
    out_specs = (
        P(None, None, "tile", None),
        P(None, None, "tile", None),
        P("lvl", None, None, None, "tile", None),
    )
    return jax.shard_map(local, mesh=mesh, in_specs=in_specs, out_specs=out_specs, check_vma=False)
```

```python
import functools
import math

import jax
import jax.numpy as jnp
from jax import lax
from jax.experimental import pallas as pl
from jax.experimental.pallas import tpu as pltpu
from jax.sharding import PartitionSpec as P

STEP_TIME = 0.25
SPRING_LIMIT = 10.0
RADIUS_CAP = 3.0
VISCOSITY = 0.5
POLYMER_WEIGHT = 0.2
NOISE_GAIN = math.sqrt(STEP_TIME / 2.0)
PLANES = 4
SAMPLES = 8
PAIRS = ((0, 0), (1, 1), (2, 2), (0, 1), (0, 2), (1, 2))
RIM = (3, 1, 5)
REST = (0, 2, 4)
F32 = jnp.float32
ANY = pl.BlockSpec(memory_space=pl.ANY)
VMEM = pl.BlockSpec(memory_space=pltpu.VMEM)


def view(field):
    lead = field.shape[:-2]
    split = field.reshape(lead + (4, 4, 128))
    return jnp.swapaxes(split, -3, -2).reshape(lead + (16, 128))


def unview(field):
    lead = field.shape[:-2]
    split = field.reshape(lead + (4, 4, 128))
    return jnp.swapaxes(split, -3, -2).reshape(lead + (4, 512))


def row_of():
    return lax.rem(lax.broadcasted_iota(jnp.int32, (16, 128), 0), 4)


def lane_of():
    return lax.broadcasted_iota(jnp.int32, (16, 128), 1)


def column_pair(cells, lane):
    after = pltpu.roll(jnp.where(lane == 0, pltpu.roll(cells, 12, 0), cells), 127, 1)
    before = pltpu.roll(jnp.where(lane == 127, pltpu.roll(cells, 4, 0), cells), 1, 1)
    return after, before


def row_pair(cells, following, preceding, row):
    after = jnp.where(row == 3, pltpu.roll(following, 3, 0), pltpu.roll(cells, 15, 0))
    before = jnp.where(row == 0, pltpu.roll(preceding, 13, 0), pltpu.roll(cells, 1, 0))
    return after, before


def plane_pair(planes, p):
    zero = jnp.zeros_like(planes[0])
    after = planes[p + 1] if p + 1 < PLANES else zero
    before = planes[p - 1] if p > 0 else zero
    return after, before


def neighbours(core, mate, far):
    at_first = core == 0
    following = [jnp.where(at_first, m, f) for m, f in zip(mate, far)]
    preceding = [jnp.where(at_first, f, m) for m, f in zip(mate, far)]
    return following, preceding


def quad_sum(cells, row, lane):
    even_row = lax.rem(row, 2) == 0
    cells = cells + jnp.where(even_row, pltpu.roll(cells, 15, 0), pltpu.roll(cells, 1, 0))
    even_lane = lax.rem(lane, 2) == 0
    return cells + jnp.where(even_lane, pltpu.roll(cells, 127, 1), pltpu.roll(cells, 1, 1))


def spring_of(state):
    return 1.0 / (
        1.0
        - (state[0] * state[0] + state[1] * state[1] + state[2] * state[2]) * (1.0 / SPRING_LIMIT)
    )


def applied(kappa, state):
    return [kappa[a][0] * state[0] + kappa[a][1] * state[1] + kappa[a][2] * state[2] for a in range(3)]


def capped(moved):
    length2 = moved[0] * moved[0] + moved[1] * moved[1] + moved[2] * moved[2]
    factor = jnp.minimum(1.0, RADIUS_CAP * lax.rsqrt(jnp.maximum(length2, RADIUS_CAP * RADIUS_CAP)))
    return [entry * factor for entry in moved]


def moments(state):
    spring = spring_of(state)
    scaled = [spring * state[a] for a in range(3)]
    return [scaled[a] * state[b] for a, b in PAIRS]


def prepare_kernel(state, noise, here, whole, first, later, bring, state_sem, noise_sem):
    level = lax.axis_index("lvl")

    def copies(s):
        return (
            pltpu.make_async_copy(state.at[:, s], here.at[:, s], state_sem.at[s]),
            pltpu.make_async_copy(noise.at[:, :, s], bring.at[:, :, s], noise_sem.at[s]),
        )

    for s in range(SAMPLES):
        for copy in copies(s):
            copy.start()

    def body(s, carry):
        for copy in copies(s):
            copy.wait()
        for p in range(PLANES):
            q = [here[a, s, p] for a in range(3)]
            xa = [NOISE_GAIN * bring[0, a, s, p].astype(F32) for a in range(3)]
            xb = [NOISE_GAIN * bring[1, a, s, p].astype(F32) for a in range(3)]
            spring = spring_of(q)
            keep = 1.0 - (0.5 * STEP_TIME) * spring
            for a in range(3):
                whole[a, s, p] = keep * q[a] + (xa[a] + xb[a])

            @pl.when(level != 0)
            def _():
                keep = 1.0 - (0.25 * STEP_TIME) * spring
                for a in range(3):
                    first[a, s, p] = keep * q[a] + xa[a]
                    later[a, s, p] = xb[a]

        return carry

    lax.fori_loop(0, SAMPLES, body, 0)


def advance_kernel(vel, mate, far, state, whole, first, later, moved, part, toward, rest):
    level = lax.axis_index("lvl")
    core = lax.rem(lax.axis_index("tile"), 2)
    row, lane = row_of(), lane_of()
    velocity = [[vel[a, p] for p in range(PLANES)] for a in range(3)]

    def gradient(p):
        result = []
        for a in range(3):
            following, preceding = neighbours(core, [mate[a, p]], [far[a, p]])
            pairs = (
                plane_pair(velocity[a], p),
                row_pair(velocity[a][p], following[0], preceding[0], row),
                column_pair(velocity[a][p], lane),
            )
            result.append([(after - before) * 0.5 for after, before in pairs])
        return result

    def emit(p, values):
        for c in range(6):
            part[c, p] = values[c]

    @pl.when(level == 0)
    def _():
        for p in range(PLANES):
            kappa = [[STEP_TIME * entry for entry in line] for line in gradient(p)]

            def body(s, sums, p=p, kappa=kappa):
                pull = applied(kappa, [state[a, s, p] for a in range(3)])
                out = capped([whole[a, s, p] + pull[a] for a in range(3)])
                for a in range(3):
                    moved[a, s, p] = out[a]
                return tuple(t + m for t, m in zip(sums, moments(out)))

            sums = lax.fori_loop(0, SAMPLES, body, (jnp.zeros((16, 128), F32),) * 6, unroll=2)
            emit(p, [t * (1.0 / SAMPLES) - (1.0 if c < 3 else 0.0) for c, t in enumerate(sums)])

    @pl.when(level != 0)
    def _():
        for pair in range(PLANES // 2):
            lower, upper = gradient(2 * pair), gradient(2 * pair + 1)
            kappa = [
                [quad_sum(lower[a][b] + upper[a][b], row, lane) * (0.125 * 0.5 * STEP_TIME) for b in range(3)]
                for a in range(3)
            ]

            def body(s, sums, pair=pair, kappa=kappa):
                for p in (2 * pair, 2 * pair + 1):
                    pull = applied(kappa, [state[a, s, p] for a in range(3)])
                    coarse = capped([whole[a, s, p] + 2.0 * pull[a] for a in range(3)])
                    half = capped([first[a, s, p] + pull[a] for a in range(3)])
                    pull = applied(kappa, half)
                    keep = 1.0 - (0.25 * STEP_TIME) * spring_of(half)
                    fine = capped([keep * half[a] + pull[a] + later[a, s, p] for a in range(3)])
                    for a in range(3):
                        moved[a, s, p] = fine[a]
                    sums = tuple(
                        t + (f - c) for t, f, c in zip(sums, moments(fine), moments(coarse))
                    )
                return sums

            sums = lax.fori_loop(0, SAMPLES, body, (jnp.zeros((16, 128), F32),) * 6)
            values = [quad_sum(t, row, lane) * (1.0 / 64.0) for t in sums]
            emit(2 * pair, values)
            emit(2 * pair + 1, values)

    far_row = core * 3
    for i, c in enumerate(RIM):
        for p in range(PLANES):
            toward[0, i, p] = part[c, p, pl.ds(far_row, 4, stride=4), :]
            toward[1, i, p] = part[c, p, pl.ds(3 - far_row, 4, stride=4), :]
            rest[i, p, 16:20] = part[c, p, pl.ds(1, 4, stride=4), :]
            rest[i, p, 20:24] = part[c, p, pl.ds(2, 4, stride=4), :]
    for i, c in enumerate(REST):
        for p in range(PLANES):
            rest[i, p, 0:16] = part[c, p]


def momentum_kernel(vel, mate, far, moved, solvent, stored, sem):
    copy = pltpu.make_async_copy(moved, stored, sem)
    copy.start()
    core = lax.rem(lax.axis_index("tile"), 2)
    row, lane = row_of(), lane_of()
    velocity = [[vel[a, p] for p in range(PLANES)] for a in range(3)]
    for p in range(PLANES):
        for a in range(3):
            following, preceding = neighbours(core, [mate[a, p]], [far[a, p]])
            here = velocity[a][p]
            pairs = (
                plane_pair(velocity[a], p),
                row_pair(here, following[0], preceding[0], row),
                column_pair(here, lane),
            )
            laplace = -6.0 * here
            carried = jnp.zeros_like(here)
            for b, (after, before) in enumerate(pairs):
                laplace = laplace + (after + before)
                carried = carried + velocity[b][p] * ((after - before) * 0.5)
            solvent[a, p] = here + STEP_TIME * (VISCOSITY * laplace - carried)
    copy.wait()


def over_runs(rows):
    return jnp.concatenate([jnp.broadcast_to(rows[j : j + 1], (4, 128)) for j in range(4)], axis=0)


def final_kernel(solvent, part, rest, edges, from_far, from_mate, velocity_next, stress):
    core = lax.rem(lax.axis_index("tile"), 2)
    row, lane = row_of(), lane_of()
    far_row = core * 3
    for i, c in enumerate(RIM):
        for p in range(PLANES):
            stress[c, p, pl.ds(far_row, 4, stride=4), :] = edges[0, i, p]
            stress[c, p, pl.ds(3 - far_row, 4, stride=4), :] = edges[1, i, p]
            for r in (1, 2):
                own = part[c, p, pl.ds(r, 4, stride=4), :]
                stress[c, p, pl.ds(r, 4, stride=4), :] = own + rest[i, p, 12 + 4 * r : 16 + 4 * r]
    for i, c in enumerate(REST):
        for p in range(PLANES):
            stress[c, p] = part[c, p] + rest[i, p, 0:16]
    walls = [[stress[c, p] for p in range(PLANES)] for c in (0, 3, 4)]
    for p in range(PLANES):
        for a in range(3):
            following, preceding = neighbours(core, [over_runs(from_mate[a, p])], [over_runs(from_far[a, p])])
            rim = stress[RIM[a], p]
            y_after = jnp.where(row == 3, following[0], pltpu.roll(rim, 15, 0))
            y_before = jnp.where(row == 0, preceding[0], pltpu.roll(rim, 1, 0))
            x_after, x_before = plane_pair(walls[a], p)
            z_after, z_before = column_pair(stress[(4, 5, 2)[a], p], lane)
            force = (x_after - x_before) * 0.5 + (y_after - y_before) * 0.5 + (z_after - z_before) * 0.5
            velocity_next[a, p] = solvent[a, p] + (STEP_TIME * POLYMER_WEIGHT) * force


def limit(mebibytes):
    return pltpu.CompilerParams(vmem_limit_bytes=mebibytes * 2**20)


def shape(*extent):
    return jax.ShapeDtypeStruct(extent, F32)


def far_pairs(tiles):
    pairs = []
    for l in range(2):
        for t in range(1, tiles, 2):
            u = (t + 1) % tiles
            m = 1 - l if (t // 8) % 4 == 3 and t % 8 == 7 else l
            pairs += [(l * tiles + t, m * tiles + u), (m * tiles + u, l * tiles + t)]
    return pairs


def local(velocity, dumbbells, increments):
    tiles = lax.axis_size("tile")
    far_swap = far_pairs(tiles)
    mate_swap = [(t, t ^ 1) for t in range(tiles)]
    level_swap = [(0, 1), (1, 0)]
    vel = view(velocity)
    far = lax.ppermute(vel, ("lvl", "tile"), far_swap)
    mate = lax.ppermute(vel, "tile", mate_swap)
    field = (3, PLANES, 16, 128)
    ensemble = (3, SAMPLES, PLANES, 16, 128)
    here, whole, first, later = pl.pallas_call(
        prepare_kernel,
        out_shape=[shape(*ensemble)] * 4,
        in_specs=[ANY] * 2,
        out_specs=[VMEM] * 4,
        scratch_shapes=[
            pltpu.VMEM((2,) + ensemble, jnp.bfloat16),
            pltpu.SemaphoreType.DMA((SAMPLES,)),
            pltpu.SemaphoreType.DMA((SAMPLES,)),
        ],
        compiler_params=limit(16),
    )(view(dumbbells[0]), view(increments[0]))
    moved, part, toward, rest = pl.pallas_call(
        advance_kernel,
        out_shape=[shape(*ensemble), shape(6, PLANES, 16, 128), shape(2, 3, PLANES, 4, 128), shape(3, PLANES, 24, 128)],
        in_specs=[VMEM] * 7,
        out_specs=[VMEM] * 4,
        compiler_params=limit(16),
    )(vel, mate, far, here, whole, first, later)
    toward_other = lax.ppermute(toward, "lvl", level_swap)
    rest_other = lax.ppermute(rest, "lvl", level_swap)
    edges = toward + toward_other
    from_far = lax.ppermute(edges[0], ("lvl", "tile"), far_swap)
    from_mate = lax.ppermute(edges[1], "tile", mate_swap)
    solvent, stored = pl.pallas_call(
        momentum_kernel,
        out_shape=[shape(*field), shape(*ensemble)],
        in_specs=[VMEM] * 3 + [ANY],
        out_specs=[VMEM, ANY],
        scratch_shapes=[pltpu.SemaphoreType.DMA],
        compiler_params=limit(8),
    )(vel, mate, far, moved)
    velocity_next, stress = pl.pallas_call(
        final_kernel,
        out_shape=[shape(*field), shape(6, PLANES, 16, 128)],
        in_specs=[VMEM] * 6,
        out_specs=[VMEM] * 2,
        compiler_params=limit(8),
    )(solvent, part, rest_other, edges, from_far, from_mate)
    return (unview(velocity_next), unview(stress), unview(stored)[None])


def solution(mesh):
    in_specs = (
        P(None, None, "tile", None),
        P("lvl", None, None, None, "tile", None),
        P("lvl", None, None, None, None, "tile", None),
    )
    out_specs = (
        P(None, None, "tile", None),
        P(None, None, "tile", None),
        P("lvl", None, None, None, "tile", None),
    )
    return jax.shard_map(local, mesh=mesh, in_specs=in_specs, out_specs=out_specs, check_vma=False)
```

```python
import functools
import math

import jax
import jax.numpy as jnp
from jax import lax
from jax.experimental import pallas as pl
from jax.experimental.pallas import tpu as pltpu
from jax.sharding import PartitionSpec as P

STEP_TIME = 0.25
SPRING_LIMIT = 10.0
RADIUS_CAP = 3.0
VISCOSITY = 0.5
POLYMER_WEIGHT = 0.2
NOISE_GAIN = math.sqrt(STEP_TIME / 2.0)
PLANES = 4
SAMPLES = 8
PAIRS = ((0, 0), (1, 1), (2, 2), (0, 1), (0, 2), (1, 2))
RIM = (3, 1, 5)
REST = (0, 2, 4)
F32 = jnp.float32
ANY = pl.BlockSpec(memory_space=pl.ANY)
VMEM = pl.BlockSpec(memory_space=pltpu.VMEM)


def view(field):
    lead = field.shape[:-2]
    split = field.reshape(lead + (4, 4, 128))
    return jnp.swapaxes(split, -3, -2).reshape(lead + (16, 128))


def unview(field):
    lead = field.shape[:-2]
    split = field.reshape(lead + (4, 4, 128))
    return jnp.swapaxes(split, -3, -2).reshape(lead + (4, 512))


def row_of():
    return lax.rem(lax.broadcasted_iota(jnp.int32, (16, 128), 0), 4)


def lane_of():
    return lax.broadcasted_iota(jnp.int32, (16, 128), 1)


def column_pair(cells, lane):
    after = pltpu.roll(jnp.where(lane == 0, pltpu.roll(cells, 12, 0), cells), 127, 1)
    before = pltpu.roll(jnp.where(lane == 127, pltpu.roll(cells, 4, 0), cells), 1, 1)
    return after, before


def row_pair(cells, edges, row):
    following, preceding = edges
    after = jnp.where(row == 3, following, pltpu.roll(cells, 15, 0))
    before = jnp.where(row == 0, preceding, pltpu.roll(cells, 1, 0))
    return after, before


def plane_pair(planes, p):
    zero = jnp.zeros_like(planes[0])
    after = planes[p + 1] if p + 1 < PLANES else zero
    before = planes[p - 1] if p > 0 else zero
    return after, before


def over_runs(rows):
    return jnp.concatenate([jnp.broadcast_to(rows[j : j + 1], (4, 128)) for j in range(4)], axis=0)


def block_edges(core, mate, far):
    rows = over_runs(far)
    following = jnp.where(core == 0, pltpu.roll(mate, 3, 0), rows)
    preceding = jnp.where(core == 0, rows, pltpu.roll(mate, 13, 0))
    return following, preceding


def row_edges(core, mate, far):
    mate, far = over_runs(mate), over_runs(far)
    return jnp.where(core == 0, mate, far), jnp.where(core == 0, far, mate)


def quad_sum(cells, row, lane):
    even_row = lax.rem(row, 2) == 0
    cells = cells + jnp.where(even_row, pltpu.roll(cells, 15, 0), pltpu.roll(cells, 1, 0))
    even_lane = lax.rem(lane, 2) == 0
    return cells + jnp.where(even_lane, pltpu.roll(cells, 127, 1), pltpu.roll(cells, 1, 1))


def spring_of(state):
    length2 = state[0] * state[0] + state[1] * state[1] + state[2] * state[2]
    slack = 1.0 - length2 * (1.0 / SPRING_LIMIT)
    guess = pl.reciprocal(slack, approx=True)
    return guess * (2.0 - slack * guess)


def applied(kappa, state):
    return [kappa[a][0] * state[0] + kappa[a][1] * state[1] + kappa[a][2] * state[2] for a in range(3)]


def capped(moved):
    length2 = moved[0] * moved[0] + moved[1] * moved[1] + moved[2] * moved[2]
    factor = jnp.minimum(1.0, RADIUS_CAP * lax.rsqrt(jnp.maximum(length2, RADIUS_CAP * RADIUS_CAP)))
    return [entry * factor for entry in moved]


def moments(state):
    spring = spring_of(state)
    scaled = [spring * state[a] for a in range(3)]
    return [scaled[a] * state[b] for a, b in PAIRS]


def edge_kernel(vel, toward_far):
    far_row = 3 * lax.rem(lax.axis_index("tile"), 2)
    for a in range(3):
        for p in range(PLANES):
            toward_far[a, p] = vel[a, p, pl.ds(far_row, 4, stride=4), :]


def prepare_kernel(state, noise, here, whole, first, later, bring, state_sem, noise_sem):
    level = lax.axis_index("lvl")

    def copies(s):
        return (
            pltpu.make_async_copy(state.at[:, s], here.at[:, s], state_sem.at[s]),
            pltpu.make_async_copy(noise.at[:, :, s], bring.at[:, :, s], noise_sem.at[s]),
        )

    for s in range(SAMPLES):
        for copy in copies(s):
            copy.start()

    def body(s, carry):
        for copy in copies(s):
            copy.wait()
        for p in range(PLANES):
            q = [here[a, s, p] for a in range(3)]
            xa = [NOISE_GAIN * bring[0, a, s, p].astype(F32) for a in range(3)]
            xb = [NOISE_GAIN * bring[1, a, s, p].astype(F32) for a in range(3)]
            spring = spring_of(q)
            keep = 1.0 - (0.5 * STEP_TIME) * spring
            for a in range(3):
                whole[a, s, p] = keep * q[a] + (xa[a] + xb[a])

            @pl.when(level != 0)
            def _():
                keep = 1.0 - (0.25 * STEP_TIME) * spring
                for a in range(3):
                    first[a, s, p] = keep * q[a] + xa[a]
                    later[a, s, p] = xb[a]

        return carry

    lax.fori_loop(0, SAMPLES, body, 0)


def advance_kernel(vel, mate, far, state, whole, first, later, moved, part, toward, packed):
    level = lax.axis_index("lvl")
    core = lax.rem(lax.axis_index("tile"), 2)
    row, lane = row_of(), lane_of()
    velocity = [[vel[a, p] for p in range(PLANES)] for a in range(3)]

    def gradient(p):
        result = []
        for a in range(3):
            pairs = (
                plane_pair(velocity[a], p),
                row_pair(velocity[a][p], block_edges(core, mate[a, p], far[a, p]), row),
                column_pair(velocity[a][p], lane),
            )
            result.append([(after - before) * 0.5 for after, before in pairs])
        return result

    def emit(p, values):
        for c in range(6):
            part[c, p] = values[c]

    @pl.when(level == 0)
    def _():
        for p in range(PLANES):
            kappa = [[STEP_TIME * entry for entry in line] for line in gradient(p)]

            def body(s, sums, p=p, kappa=kappa):
                pull = applied(kappa, [state[a, s, p] for a in range(3)])
                out = capped([whole[a, s, p] + pull[a] for a in range(3)])
                for a in range(3):
                    moved[a, s, p] = out[a]
                return tuple(t + m for t, m in zip(sums, moments(out)))

            sums = lax.fori_loop(0, SAMPLES, body, (jnp.zeros((16, 128), F32),) * 6, unroll=2)
            emit(p, [t * (1.0 / SAMPLES) - (1.0 if c < 3 else 0.0) for c, t in enumerate(sums)])

    @pl.when(level != 0)
    def _():
        for pair in range(PLANES // 2):
            lower, upper = gradient(2 * pair), gradient(2 * pair + 1)
            kappa = [
                [quad_sum(lower[a][b] + upper[a][b], row, lane) * (0.125 * 0.5 * STEP_TIME) for b in range(3)]
                for a in range(3)
            ]

            def body(s, sums, pair=pair, kappa=kappa):
                for p in (2 * pair, 2 * pair + 1):
                    pull = applied(kappa, [state[a, s, p] for a in range(3)])
                    coarse = capped([whole[a, s, p] + 2.0 * pull[a] for a in range(3)])
                    half = capped([first[a, s, p] + pull[a] for a in range(3)])
                    pull = applied(kappa, half)
                    keep = 1.0 - (0.25 * STEP_TIME) * spring_of(half)
                    fine = capped([keep * half[a] + pull[a] + later[a, s, p] for a in range(3)])
                    for a in range(3):
                        moved[a, s, p] = fine[a]
                    sums = tuple(
                        t + (f - c) for t, f, c in zip(sums, moments(fine), moments(coarse))
                    )
                return sums

            sums = lax.fori_loop(0, SAMPLES, body, (jnp.zeros((16, 128), F32),) * 6)
            values = [quad_sum(t, row, lane) * (1.0 / 64.0) for t in sums]
            emit(2 * pair, values)
            emit(2 * pair + 1, values)

    far_row = core * 3
    for i, c in enumerate(RIM):
        for p in range(PLANES):
            toward[0, i, p] = part[c, p, pl.ds(far_row, 4, stride=4), :]
            toward[1, i, p] = part[c, p, pl.ds(3 - far_row, 4, stride=4), :]

    for e in range(2):
        for i in range(3):
            for p in range(PLANES):
                packed[(e * 3 + i) * PLANES + p] = toward[e, i, p]

    @pl.when(level == 0)
    def _():
        for i, c in enumerate(RIM):
            for p in range(PLANES):
                for r in (1, 2):
                    packed[23 + (i * PLANES + p) * 2 + r] = part[c, p, pl.ds(r, 4, stride=4), :]

    @pl.when(level != 0)
    def _():
        for g in range(2):
            for c in range(6):
                for pair in range(PLANES // 2):
                    packed[24 + (g * 6 + c) * 2 + pair] = part[c, 2 * pair, pl.ds(2 * g, 4, stride=4), :]


def momentum_kernel(vel, mate, far, moved, part, solvent, stored, rest, sem):
    copy = pltpu.make_async_copy(moved, stored, sem)
    copy.start()
    for i, c in enumerate(REST):
        for p in range(PLANES):
            rest[i, p] = part[c, p]
    core = lax.rem(lax.axis_index("tile"), 2)
    row, lane = row_of(), lane_of()
    velocity = [[vel[a, p] for p in range(PLANES)] for a in range(3)]
    for p in range(PLANES):
        for a in range(3):
            here = velocity[a][p]
            pairs = (
                plane_pair(velocity[a], p),
                row_pair(here, block_edges(core, mate[a, p], far[a, p]), row),
                column_pair(here, lane),
            )
            laplace = -6.0 * here
            carried = jnp.zeros_like(here)
            for b, (after, before) in enumerate(pairs):
                laplace = laplace + (after + before)
                carried = carried + velocity[b][p] * ((after - before) * 0.5)
            solvent[a, p] = here + STEP_TIME * (VISCOSITY * laplace - carried)
    copy.wait()


def final_kernel(solvent, part, packed, rest, edges, from_far, from_mate, velocity_next, stress):
    level = lax.axis_index("lvl")
    core = lax.rem(lax.axis_index("tile"), 2)
    row, lane = row_of(), lane_of()
    far_row = core * 3

    @pl.when(level == 0)
    def _():
        for c in range(6):
            for pair in range(PLANES // 2):
                place = 24 + c * 2 + pair
                added = jnp.where(row < 2, over_runs(packed[place]), over_runs(packed[12 + place]))
                for p in (2 * pair, 2 * pair + 1):
                    stress[c, p] = part[c, p] + added

    @pl.when(level != 0)
    def _():
        for i, c in enumerate(RIM):
            for p in range(PLANES):
                stress[c, p, pl.ds(far_row, 4, stride=4), :] = edges[0, i, p]
                stress[c, p, pl.ds(3 - far_row, 4, stride=4), :] = edges[1, i, p]
                for r in (1, 2):
                    own = part[c, p, pl.ds(r, 4, stride=4), :]
                    stress[c, p, pl.ds(r, 4, stride=4), :] = own + packed[23 + (i * PLANES + p) * 2 + r]
        for i, c in enumerate(REST):
            for p in range(PLANES):
                stress[c, p] = part[c, p] + rest[i, p]

    walls = [[stress[c, p] for p in range(PLANES)] for c in (0, 3, 4)]
    for p in range(PLANES):
        for a in range(3):
            y_after, y_before = row_pair(
                stress[RIM[a], p], row_edges(core, from_mate[a, p], from_far[a, p]), row
            )
            x_after, x_before = plane_pair(walls[a], p)
            z_after, z_before = column_pair(stress[(4, 5, 2)[a], p], lane)
            force = (x_after - x_before) * 0.5 + (y_after - y_before) * 0.5 + (z_after - z_before) * 0.5
            velocity_next[a, p] = solvent[a, p] + (STEP_TIME * POLYMER_WEIGHT) * force


def limit(mebibytes):
    return pltpu.CompilerParams(vmem_limit_bytes=int(mebibytes * 2**20))


def shape(*extent):
    return jax.ShapeDtypeStruct(extent, F32)


def far_pairs(tiles, across):
    pairs = []
    for l in range(2):
        for t in range(1, tiles, 2):
            u = (t + 1) % tiles
            m = 1 - l if across and (t // 8) % 4 == 3 and t % 8 == 7 else l
            pairs += [(l * tiles + t, m * tiles + u), (m * tiles + u, l * tiles + t)]
    return pairs


def local(velocity, dumbbells, increments):
    tiles = lax.axis_size("tile")
    far_swap = far_pairs(tiles, False)
    rim_swap = far_pairs(tiles, True)
    mate_swap = [(t, t ^ 1) for t in range(tiles)]
    level_swap = [(0, 1), (1, 0)]
    vel = view(velocity)
    toward_far = pl.pallas_call(
        edge_kernel,
        out_shape=shape(3, PLANES, 4, 128),
        in_specs=[VMEM],
        out_specs=VMEM,
        compiler_params=limit(2),
    )(vel)
    far = lax.ppermute(toward_far, ("lvl", "tile"), far_swap)
    mate = lax.ppermute(vel, "tile", mate_swap)
    field = (3, PLANES, 16, 128)
    ensemble = (3, SAMPLES, PLANES, 16, 128)
    here, whole, first, later = pl.pallas_call(
        prepare_kernel,
        out_shape=[shape(*ensemble)] * 4,
        in_specs=[ANY] * 2,
        out_specs=[VMEM] * 4,
        scratch_shapes=[
            pltpu.VMEM((2,) + ensemble, jnp.bfloat16),
            pltpu.SemaphoreType.DMA((SAMPLES,)),
            pltpu.SemaphoreType.DMA((SAMPLES,)),
        ],
        compiler_params=limit(50.5),
    )(view(dumbbells[0]), view(increments[0]))
    moved, part, toward, packed = pl.pallas_call(
        advance_kernel,
        out_shape=[
            shape(*ensemble),
            shape(6, PLANES, 16, 128),
            shape(2, 3, PLANES, 4, 128),
            shape(48, 4, 128),
        ],
        in_specs=[VMEM] * 7,
        out_specs=[VMEM] * 4,
        compiler_params=limit(16),
    )(vel, mate, far, here, whole, first, later)
    packed_other = lax.ppermute(packed, "lvl", level_swap)
    solvent, stored, rest = pl.pallas_call(
        momentum_kernel,
        out_shape=[shape(*field), shape(*ensemble), shape(*field)],
        in_specs=[VMEM] * 3 + [ANY, VMEM],
        out_specs=[VMEM, ANY, VMEM],
        scratch_shapes=[pltpu.SemaphoreType.DMA],
        compiler_params=limit(8),
    )(vel, mate, far, moved, part)
    rest_other = lax.ppermute(rest, "lvl", [(0, 1)])
    edges = toward + packed_other[:24].reshape(toward.shape)
    from_far = lax.ppermute(edges[0], ("lvl", "tile"), rim_swap)
    from_mate = lax.ppermute(edges[1], "tile", mate_swap)
    velocity_next, stress = pl.pallas_call(
        final_kernel,
        out_shape=[shape(*field), shape(6, PLANES, 16, 128)],
        in_specs=[VMEM] * 7,
        out_specs=[VMEM] * 2,
        compiler_params=limit(8),
    )(solvent, part, packed_other, rest_other, edges, from_far, from_mate)
    return (unview(velocity_next), unview(stress), unview(stored)[None])


def solution(mesh):
    in_specs = (
        P(None, None, "tile", None),
        P("lvl", None, None, None, "tile", None),
        P("lvl", None, None, None, None, "tile", None),
    )
    out_specs = (
        P(None, None, "tile", None),
        P(None, None, "tile", None),
        P("lvl", None, None, None, "tile", None),
    )
    return jax.shard_map(local, mesh=mesh, in_specs=in_specs, out_specs=out_specs, check_vma=False)
```

```python
import functools
import math

import jax
import jax.numpy as jnp
from jax import lax
from jax.experimental import pallas as pl
from jax.experimental.pallas import tpu as pltpu
from jax.sharding import PartitionSpec as P

STEP_TIME = 0.25
SPRING_LIMIT = 10.0
RADIUS_CAP = 3.0
VISCOSITY = 0.5
POLYMER_WEIGHT = 0.2
NOISE_GAIN = math.sqrt(STEP_TIME / 2.0)
PLANES = 4
SAMPLES = 8
PAIRS = ((0, 0), (1, 1), (2, 2), (0, 1), (0, 2), (1, 2))
RIM = (3, 1, 5)
REST = (0, 2, 4)
F32 = jnp.float32
ANY = pl.BlockSpec(memory_space=pl.ANY)
VMEM = pl.BlockSpec(memory_space=pltpu.VMEM)


def view(field):
    lead = field.shape[:-2]
    split = field.reshape(lead + (4, 4, 128))
    return jnp.swapaxes(split, -3, -2).reshape(lead + (16, 128))


def unview(field):
    lead = field.shape[:-2]
    split = field.reshape(lead + (4, 4, 128))
    return jnp.swapaxes(split, -3, -2).reshape(lead + (4, 512))


def row_of():
    return lax.rem(lax.broadcasted_iota(jnp.int32, (16, 128), 0), 4)


def lane_of():
    return lax.broadcasted_iota(jnp.int32, (16, 128), 1)


def column_pair(cells, lane):
    after = pltpu.roll(jnp.where(lane == 0, pltpu.roll(cells, 12, 0), cells), 127, 1)
    before = pltpu.roll(jnp.where(lane == 127, pltpu.roll(cells, 4, 0), cells), 1, 1)
    return after, before


def row_pair(cells, edges, row):
    following, preceding = edges
    after = jnp.where(row == 3, following, pltpu.roll(cells, 15, 0))
    before = jnp.where(row == 0, preceding, pltpu.roll(cells, 1, 0))
    return after, before


def plane_pair(planes, p):
    zero = jnp.zeros_like(planes[0])
    after = planes[p + 1] if p + 1 < PLANES else zero
    before = planes[p - 1] if p > 0 else zero
    return after, before


def over_runs(rows):
    return jnp.concatenate([jnp.broadcast_to(rows[j : j + 1], (4, 128)) for j in range(4)], axis=0)


def block_edges(core, mate, far):
    rows = over_runs(far)
    following = jnp.where(core == 0, pltpu.roll(mate, 3, 0), rows)
    preceding = jnp.where(core == 0, rows, pltpu.roll(mate, 13, 0))
    return following, preceding


def beyond(edges, row):
    following, preceding = edges
    return jnp.where(row == 3, following, 0.0) - jnp.where(row == 0, preceding, 0.0)


def row_edges(core, mate, far):
    mate, far = over_runs(mate), over_runs(far)
    return jnp.where(core == 0, mate, far), jnp.where(core == 0, far, mate)


def quad_sum(cells, row, lane):
    even_row = lax.rem(row, 2) == 0
    cells = cells + jnp.where(even_row, pltpu.roll(cells, 15, 0), pltpu.roll(cells, 1, 0))
    even_lane = lax.rem(lane, 2) == 0
    return cells + jnp.where(even_lane, pltpu.roll(cells, 127, 1), pltpu.roll(cells, 1, 1))


def spring_of(state):
    length2 = state[0] * state[0] + state[1] * state[1] + state[2] * state[2]
    slack = 1.0 - length2 * (1.0 / SPRING_LIMIT)
    guess = pl.reciprocal(slack, approx=True)
    return guess * (2.0 - slack * guess)


def applied(kappa, state):
    return [kappa[a][0] * state[0] + kappa[a][1] * state[1] + kappa[a][2] * state[2] for a in range(3)]


def capped(moved):
    length2 = moved[0] * moved[0] + moved[1] * moved[1] + moved[2] * moved[2]
    factor = jnp.minimum(1.0, RADIUS_CAP * lax.rsqrt(jnp.maximum(length2, RADIUS_CAP * RADIUS_CAP)))
    return [entry * factor for entry in moved]


def moments(state):
    spring = spring_of(state)
    scaled = [spring * state[a] for a in range(3)]
    return [scaled[a] * state[b] for a, b in PAIRS]


def edge_kernel(vel, toward_far):
    far_row = 3 * lax.rem(lax.axis_index("tile"), 2)
    for a in range(3):
        for p in range(PLANES):
            toward_far[a, p] = vel[a, p, pl.ds(far_row, 4, stride=4), :]


def prepare_kernel(state, noise, vel, here, whole, first, later, slopes, bring, state_sem, noise_sem):
    level = lax.axis_index("lvl")

    def copies(s):
        return (
            pltpu.make_async_copy(state.at[:, s], here.at[:, s], state_sem.at[s]),
            pltpu.make_async_copy(noise.at[:, :, s], bring.at[:, :, s], noise_sem.at[s]),
        )

    for s in range(SAMPLES):
        for copy in copies(s):
            copy.start()

    row, lane = row_of(), lane_of()
    velocity = [[vel[a, p] for p in range(PLANES)] for a in range(3)]
    nothing = jnp.zeros((16, 128), F32)

    def differences(a, p):
        pairs = (
            plane_pair(velocity[a], p),
            row_pair(velocity[a][p], (nothing, nothing), row),
            column_pair(velocity[a][p], lane),
        )
        return [(after - before) * 0.5 for after, before in pairs]

    @pl.when(level == 0)
    def _():
        for a in range(3):
            for p in range(PLANES):
                for b, entry in enumerate(differences(a, p)):
                    slopes[a, b, p] = STEP_TIME * entry

    @pl.when(level != 0)
    def _():
        for a in range(3):
            for pair in range(PLANES // 2):
                lower, upper = differences(a, 2 * pair), differences(a, 2 * pair + 1)
                for b in range(3):
                    slopes[a, b, pair] = quad_sum(lower[b] + upper[b], row, lane) * (
                        0.125 * 0.5 * STEP_TIME
                    )

    def body(s, carry):
        for copy in copies(s):
            copy.wait()
        for p in range(PLANES):
            q = [here[a, s, p] for a in range(3)]
            xa = [NOISE_GAIN * bring[0, a, s, p].astype(F32) for a in range(3)]
            xb = [NOISE_GAIN * bring[1, a, s, p].astype(F32) for a in range(3)]
            spring = spring_of(q)
            keep = 1.0 - (0.5 * STEP_TIME) * spring
            for a in range(3):
                whole[a, s, p] = keep * q[a] + (xa[a] + xb[a])

            @pl.when(level != 0)
            def _():
                keep = 1.0 - (0.25 * STEP_TIME) * spring
                for a in range(3):
                    first[a, s, p] = keep * q[a] + xa[a]
                    later[a, s, p] = xb[a]

        return carry

    lax.fori_loop(0, SAMPLES, body, 0)


def advance_kernel(slopes, mate, far, state, whole, first, later, moved, part, toward, packed):
    level = lax.axis_index("lvl")
    core = lax.rem(lax.axis_index("tile"), 2)
    row, lane = row_of(), lane_of()
    def outer(a, p):
        return beyond(block_edges(core, mate[a, p], far[a, p]), row)

    def emit(p, values):
        for c in range(6):
            part[c, p] = values[c]

    @pl.when(level == 0)
    def _():
        for p in range(PLANES):
            kappa = [[slopes[a, b, p] for b in range(3)] for a in range(3)]
            for a in range(3):
                kappa[a][1] = kappa[a][1] + (0.5 * STEP_TIME) * outer(a, p)

            def body(s, sums, p=p, kappa=kappa):
                pull = applied(kappa, [state[a, s, p] for a in range(3)])
                out = capped([whole[a, s, p] + pull[a] for a in range(3)])
                for a in range(3):
                    moved[a, s, p] = out[a]
                return tuple(t + m for t, m in zip(sums, moments(out)))

            sums = lax.fori_loop(0, SAMPLES, body, (jnp.zeros((16, 128), F32),) * 6, unroll=2)
            emit(p, [t * (1.0 / SAMPLES) - (1.0 if c < 3 else 0.0) for c, t in enumerate(sums)])

    @pl.when(level != 0)
    def _():
        for pair in range(PLANES // 2):
            kappa = [[slopes[a, b, pair] for b in range(3)] for a in range(3)]
            for a in range(3):
                edge = quad_sum(outer(a, 2 * pair) + outer(a, 2 * pair + 1), row, lane)
                kappa[a][1] = kappa[a][1] + edge * (0.5 * 0.125 * 0.5 * STEP_TIME)

            def body(s, sums, pair=pair, kappa=kappa):
                for p in (2 * pair, 2 * pair + 1):
                    pull = applied(kappa, [state[a, s, p] for a in range(3)])
                    coarse = capped([whole[a, s, p] + 2.0 * pull[a] for a in range(3)])
                    half = capped([first[a, s, p] + pull[a] for a in range(3)])
                    pull = applied(kappa, half)
                    keep = 1.0 - (0.25 * STEP_TIME) * spring_of(half)
                    fine = capped([keep * half[a] + pull[a] + later[a, s, p] for a in range(3)])
                    for a in range(3):
                        moved[a, s, p] = fine[a]
                    sums = tuple(
                        t + (f - c) for t, f, c in zip(sums, moments(fine), moments(coarse))
                    )
                return sums

            sums = lax.fori_loop(0, SAMPLES, body, (jnp.zeros((16, 128), F32),) * 6)
            values = [quad_sum(t, row, lane) * (1.0 / 64.0) for t in sums]
            emit(2 * pair, values)
            emit(2 * pair + 1, values)

    far_row = core * 3
    for i, c in enumerate(RIM):
        for p in range(PLANES):
            toward[0, i, p] = part[c, p, pl.ds(far_row, 4, stride=4), :]
            toward[1, i, p] = part[c, p, pl.ds(3 - far_row, 4, stride=4), :]

    for e in range(2):
        for i in range(3):
            for p in range(PLANES):
                packed[(e * 3 + i) * PLANES + p] = toward[e, i, p]

    @pl.when(level == 0)
    def _():
        for i, c in enumerate(RIM):
            for p in range(PLANES):
                for r in (1, 2):
                    packed[23 + (i * PLANES + p) * 2 + r] = part[c, p, pl.ds(r, 4, stride=4), :]

    @pl.when(level != 0)
    def _():
        for g in range(2):
            for c in range(6):
                for pair in range(PLANES // 2):
                    packed[24 + (g * 6 + c) * 2 + pair] = part[c, 2 * pair, pl.ds(2 * g, 4, stride=4), :]


def momentum_kernel(vel, mate, far, moved, part, solvent, stored, rest, sem):
    copy = pltpu.make_async_copy(moved, stored, sem)
    copy.start()
    for i, c in enumerate(REST):
        for p in range(PLANES):
            rest[i, p] = part[c, p]
    core = lax.rem(lax.axis_index("tile"), 2)
    row, lane = row_of(), lane_of()
    velocity = [[vel[a, p] for p in range(PLANES)] for a in range(3)]
    for p in range(PLANES):
        for a in range(3):
            here = velocity[a][p]
            pairs = (
                plane_pair(velocity[a], p),
                row_pair(here, block_edges(core, mate[a, p], far[a, p]), row),
                column_pair(here, lane),
            )
            laplace = -6.0 * here
            carried = jnp.zeros_like(here)
            for b, (after, before) in enumerate(pairs):
                laplace = laplace + (after + before)
                carried = carried + velocity[b][p] * ((after - before) * 0.5)
            solvent[a, p] = here + STEP_TIME * (VISCOSITY * laplace - carried)
    copy.wait()


def stress_kernel(solvent, part, packed, rest, edges, inner, stress):
    level = lax.axis_index("lvl")
    core = lax.rem(lax.axis_index("tile"), 2)
    row, lane = row_of(), lane_of()
    far_row = core * 3

    @pl.when(level == 0)
    def _():
        for c in range(6):
            for pair in range(PLANES // 2):
                place = 24 + c * 2 + pair
                added = jnp.where(row < 2, over_runs(packed[place]), over_runs(packed[12 + place]))
                for p in (2 * pair, 2 * pair + 1):
                    stress[c, p] = part[c, p] + added

    @pl.when(level != 0)
    def _():
        for i, c in enumerate(RIM):
            for p in range(PLANES):
                stress[c, p, pl.ds(far_row, 4, stride=4), :] = edges[0, i, p]
                stress[c, p, pl.ds(3 - far_row, 4, stride=4), :] = edges[1, i, p]
                for r in (1, 2):
                    own = part[c, p, pl.ds(r, 4, stride=4), :]
                    stress[c, p, pl.ds(r, 4, stride=4), :] = own + packed[23 + (i * PLANES + p) * 2 + r]
        for i, c in enumerate(REST):
            for p in range(PLANES):
                stress[c, p] = part[c, p] + rest[i, p]

    walls = [[stress[c, p] for p in range(PLANES)] for c in (0, 3, 4)]
    for p in range(PLANES):
        for a in range(3):
            nothing = jnp.zeros((16, 128), F32)
            y_after, y_before = row_pair(stress[RIM[a], p], (nothing, nothing), row)
            x_after, x_before = plane_pair(walls[a], p)
            z_after, z_before = column_pair(stress[(4, 5, 2)[a], p], lane)
            force = (x_after - x_before) * 0.5 + (y_after - y_before) * 0.5 + (z_after - z_before) * 0.5
            inner[a, p] = solvent[a, p] + (STEP_TIME * POLYMER_WEIGHT) * force


def final_kernel(inner, from_far, from_mate, velocity_next):
    core = lax.rem(lax.axis_index("tile"), 2)
    row = row_of()
    for p in range(PLANES):
        for a in range(3):
            outer = beyond(row_edges(core, from_mate[a, p], from_far[a, p]), row)
            velocity_next[a, p] = inner[a, p] + (0.5 * STEP_TIME * POLYMER_WEIGHT) * outer


def limit(mebibytes):
    return pltpu.CompilerParams(vmem_limit_bytes=int(mebibytes * 2**20))


def shape(*extent):
    return jax.ShapeDtypeStruct(extent, F32)


def far_pairs(tiles, across):
    pairs = []
    for l in range(2):
        for t in range(1, tiles, 2):
            u = (t + 1) % tiles
            m = 1 - l if across and (t // 8) % 4 == 3 and t % 8 == 7 else l
            pairs += [(l * tiles + t, m * tiles + u), (m * tiles + u, l * tiles + t)]
    return pairs


def local(velocity, dumbbells, increments):
    tiles = lax.axis_size("tile")
    far_swap = far_pairs(tiles, False)
    rim_swap = far_pairs(tiles, True)
    mate_swap = [(t, t ^ 1) for t in range(tiles)]
    level_swap = [(0, 1), (1, 0)]
    vel = view(velocity)
    toward_far = pl.pallas_call(
        edge_kernel,
        out_shape=shape(3, PLANES, 4, 128),
        in_specs=[VMEM],
        out_specs=VMEM,
        compiler_params=limit(2),
    )(vel)
    far = lax.ppermute(toward_far, ("lvl", "tile"), far_swap)
    mate = lax.ppermute(vel, "tile", mate_swap)
    field = (3, PLANES, 16, 128)
    ensemble = (3, SAMPLES, PLANES, 16, 128)
    here, whole, first, later, slopes = pl.pallas_call(
        prepare_kernel,
        out_shape=[shape(*ensemble)] * 4 + [shape(3, 3, PLANES, 16, 128)],
        in_specs=[ANY] * 2 + [VMEM],
        out_specs=[VMEM] * 5,
        scratch_shapes=[
            pltpu.VMEM((2,) + ensemble, jnp.bfloat16),
            pltpu.SemaphoreType.DMA((SAMPLES,)),
            pltpu.SemaphoreType.DMA((SAMPLES,)),
        ],
        compiler_params=limit(50.2),
    )(view(dumbbells[0]), view(increments[0]), vel)
    moved, part, toward, packed = pl.pallas_call(
        advance_kernel,
        out_shape=[
            shape(*ensemble),
            shape(6, PLANES, 16, 128),
            shape(2, 3, PLANES, 4, 128),
            shape(48, 4, 128),
        ],
        in_specs=[VMEM] * 7,
        out_specs=[VMEM] * 4,
        compiler_params=limit(16),
    )(slopes, mate, far, here, whole, first, later)
    packed_other = lax.ppermute(packed, "lvl", level_swap)
    solvent, stored, rest = pl.pallas_call(
        momentum_kernel,
        out_shape=[shape(*field), shape(*ensemble), shape(*field)],
        in_specs=[VMEM] * 3 + [ANY, VMEM],
        out_specs=[VMEM, ANY, VMEM],
        scratch_shapes=[pltpu.SemaphoreType.DMA],
        compiler_params=limit(8),
    )(vel, mate, far, moved, part)
    rest_other = lax.ppermute(rest, "lvl", [(0, 1)])
    edges = toward + packed_other[:24].reshape(toward.shape)
    from_far = lax.ppermute(edges[0], ("lvl", "tile"), rim_swap)
    from_mate = lax.ppermute(edges[1], "tile", mate_swap)
    inner, stress = pl.pallas_call(
        stress_kernel,
        out_shape=[shape(*field), shape(6, PLANES, 16, 128)],
        in_specs=[VMEM] * 5,
        out_specs=[VMEM] * 2,
        compiler_params=limit(8),
    )(solvent, part, packed_other, rest_other, edges)
    velocity_next = pl.pallas_call(
        final_kernel,
        out_shape=shape(*field),
        in_specs=[VMEM] * 3,
        out_specs=VMEM,
        compiler_params=limit(4),
    )(inner, from_far, from_mate)
    return (unview(velocity_next), unview(stress), unview(stored)[None])


def solution(mesh):
    in_specs = (
        P(None, None, "tile", None),
        P("lvl", None, None, None, "tile", None),
        P("lvl", None, None, None, None, "tile", None),
    )
    out_specs = (
        P(None, None, "tile", None),
        P(None, None, "tile", None),
        P("lvl", None, None, None, "tile", None),
    )
    return jax.shard_map(local, mesh=mesh, in_specs=in_specs, out_specs=out_specs, check_vma=False)
```

```python
import functools
import math

import jax
import jax.numpy as jnp
from jax import lax
from jax.experimental import pallas as pl
from jax.experimental.pallas import tpu as pltpu
from jax.sharding import PartitionSpec as P

STEP_TIME = 0.25
SPRING_LIMIT = 10.0
RADIUS_CAP = 3.0
VISCOSITY = 0.5
POLYMER_WEIGHT = 0.2
NOISE_GAIN = math.sqrt(STEP_TIME / 2.0)
PLANES = 4
SAMPLES = 8
PAIRS = ((0, 0), (1, 1), (2, 2), (0, 1), (0, 2), (1, 2))
RIM = (3, 1, 5)
REST = (0, 2, 4)
F32 = jnp.float32
ANY = pl.BlockSpec(memory_space=pl.ANY)
VMEM = pl.BlockSpec(memory_space=pltpu.VMEM)


def view(field):
    lead = field.shape[:-2]
    split = field.reshape(lead + (4, 4, 128))
    return jnp.swapaxes(split, -3, -2).reshape(lead + (16, 128))


def unview(field):
    lead = field.shape[:-2]
    split = field.reshape(lead + (4, 4, 128))
    return jnp.swapaxes(split, -3, -2).reshape(lead + (4, 512))


def row_of():
    return lax.rem(lax.broadcasted_iota(jnp.int32, (16, 128), 0), 4)


def lane_of():
    return lax.broadcasted_iota(jnp.int32, (16, 128), 1)


def column_pair(cells, lane):
    after = pltpu.roll(jnp.where(lane == 0, pltpu.roll(cells, 12, 0), cells), 127, 1)
    before = pltpu.roll(jnp.where(lane == 127, pltpu.roll(cells, 4, 0), cells), 1, 1)
    return after, before


def row_pair(cells, edges, row):
    following, preceding = edges
    after = jnp.where(row == 3, following, pltpu.roll(cells, 15, 0))
    before = jnp.where(row == 0, preceding, pltpu.roll(cells, 1, 0))
    return after, before


def plane_pair(planes, p):
    zero = jnp.zeros_like(planes[0])
    after = planes[p + 1] if p + 1 < PLANES else zero
    before = planes[p - 1] if p > 0 else zero
    return after, before


def over_runs(rows):
    return jnp.concatenate([jnp.broadcast_to(rows[j : j + 1], (4, 128)) for j in range(4)], axis=0)


def beyond(edges, row):
    following, preceding = edges
    return jnp.where(row == 3, following, 0.0) - jnp.where(row == 0, preceding, 0.0)


def row_edges(core, mate, far):
    mate, far = over_runs(mate), over_runs(far)
    return jnp.where(core == 0, mate, far), jnp.where(core == 0, far, mate)


def quad_sum(cells, row, lane):
    even_row = lax.rem(row, 2) == 0
    cells = cells + jnp.where(even_row, pltpu.roll(cells, 15, 0), pltpu.roll(cells, 1, 0))
    even_lane = lax.rem(lane, 2) == 0
    return cells + jnp.where(even_lane, pltpu.roll(cells, 127, 1), pltpu.roll(cells, 1, 1))


def spring_of(state):
    length2 = state[0] * state[0] + state[1] * state[1] + state[2] * state[2]
    slack = 1.0 - length2 * (1.0 / SPRING_LIMIT)
    guess = pl.reciprocal(slack, approx=True)
    return guess * (2.0 - slack * guess)


def applied(kappa, state):
    return [kappa[a][0] * state[0] + kappa[a][1] * state[1] + kappa[a][2] * state[2] for a in range(3)]


def capped(moved):
    length2 = moved[0] * moved[0] + moved[1] * moved[1] + moved[2] * moved[2]
    factor = jnp.minimum(1.0, RADIUS_CAP * lax.rsqrt(jnp.maximum(length2, RADIUS_CAP * RADIUS_CAP)))
    return [entry * factor for entry in moved]


def moments(state):
    spring = spring_of(state)
    scaled = [spring * state[a] for a in range(3)]
    return [scaled[a] * state[b] for a, b in PAIRS]


def edge_kernel(vel, toward_far, toward_mate):
    far_row = 3 * lax.rem(lax.axis_index("tile"), 2)
    for a in range(3):
        for p in range(PLANES):
            toward_far[a, p] = vel[a, p, pl.ds(far_row, 4, stride=4), :]
            toward_mate[a, p] = vel[a, p, pl.ds(3 - far_row, 4, stride=4), :]


def prepare_kernel(state, noise, vel, here, whole, first, later, slopes, bring, state_sem, noise_sem):
    level = lax.axis_index("lvl")

    def copies(s):
        return (
            pltpu.make_async_copy(state.at[:, s], here.at[:, s], state_sem.at[s]),
            pltpu.make_async_copy(noise.at[:, :, s], bring.at[:, :, s], noise_sem.at[s]),
        )

    for s in range(SAMPLES):
        for copy in copies(s):
            copy.start()

    row, lane = row_of(), lane_of()
    velocity = [[vel[a, p] for p in range(PLANES)] for a in range(3)]
    nothing = jnp.zeros((16, 128), F32)

    def differences(a, p):
        pairs = (
            plane_pair(velocity[a], p),
            row_pair(velocity[a][p], (nothing, nothing), row),
            column_pair(velocity[a][p], lane),
        )
        return [(after - before) * 0.5 for after, before in pairs]

    @pl.when(level == 0)
    def _():
        for a in range(3):
            for p in range(PLANES):
                for b, entry in enumerate(differences(a, p)):
                    slopes[a, b, p] = STEP_TIME * entry

    @pl.when(level != 0)
    def _():
        for a in range(3):
            for pair in range(PLANES // 2):
                lower, upper = differences(a, 2 * pair), differences(a, 2 * pair + 1)
                for b in range(3):
                    slopes[a, b, pair] = quad_sum(lower[b] + upper[b], row, lane) * (
                        0.125 * 0.5 * STEP_TIME
                    )

    def body(s, carry):
        for copy in copies(s):
            copy.wait()
        for p in range(PLANES):
            q = [here[a, s, p] for a in range(3)]
            xa = [NOISE_GAIN * bring[0, a, s, p].astype(F32) for a in range(3)]
            xb = [NOISE_GAIN * bring[1, a, s, p].astype(F32) for a in range(3)]
            spring = spring_of(q)
            keep = 1.0 - (0.5 * STEP_TIME) * spring
            for a in range(3):
                whole[a, s, p] = keep * q[a] + (xa[a] + xb[a])

            @pl.when(level != 0)
            def _():
                keep = 1.0 - (0.25 * STEP_TIME) * spring
                for a in range(3):
                    first[a, s, p] = keep * q[a] + xa[a]
                    later[a, s, p] = xb[a]

        return carry

    lax.fori_loop(0, SAMPLES, body, 0)


def advance_kernel(slopes, mate, far, state, whole, first, later, moved, part, toward, packed):
    level = lax.axis_index("lvl")
    core = lax.rem(lax.axis_index("tile"), 2)
    row, lane = row_of(), lane_of()
    def outer(a, p):
        return beyond(row_edges(core, mate[a, p], far[a, p]), row)

    def emit(p, values):
        for c in range(6):
            part[c, p] = values[c]

    @pl.when(level == 0)
    def _():
        for p in range(PLANES):
            kappa = [[slopes[a, b, p] for b in range(3)] for a in range(3)]
            for a in range(3):
                kappa[a][1] = kappa[a][1] + (0.5 * STEP_TIME) * outer(a, p)

            def body(s, sums, p=p, kappa=kappa):
                pull = applied(kappa, [state[a, s, p] for a in range(3)])
                out = capped([whole[a, s, p] + pull[a] for a in range(3)])
                for a in range(3):
                    moved[a, s, p] = out[a]
                return tuple(t + m for t, m in zip(sums, moments(out)))

            sums = lax.fori_loop(0, SAMPLES, body, (jnp.zeros((16, 128), F32),) * 6, unroll=2)
            emit(p, [t * (1.0 / SAMPLES) - (1.0 if c < 3 else 0.0) for c, t in enumerate(sums)])

    @pl.when(level != 0)
    def _():
        for pair in range(PLANES // 2):
            kappa = [[slopes[a, b, pair] for b in range(3)] for a in range(3)]
            for a in range(3):
                edge = quad_sum(outer(a, 2 * pair) + outer(a, 2 * pair + 1), row, lane)
                kappa[a][1] = kappa[a][1] + edge * (0.5 * 0.125 * 0.5 * STEP_TIME)

            def body(s, sums, pair=pair, kappa=kappa):
                for p in (2 * pair, 2 * pair + 1):
                    pull = applied(kappa, [state[a, s, p] for a in range(3)])
                    coarse = capped([whole[a, s, p] + 2.0 * pull[a] for a in range(3)])
                    half = capped([first[a, s, p] + pull[a] for a in range(3)])
                    pull = applied(kappa, half)
                    keep = 1.0 - (0.25 * STEP_TIME) * spring_of(half)
                    fine = capped([keep * half[a] + pull[a] + later[a, s, p] for a in range(3)])
                    for a in range(3):
                        moved[a, s, p] = fine[a]
                    sums = tuple(
                        t + (f - c) for t, f, c in zip(sums, moments(fine), moments(coarse))
                    )
                return sums

            sums = lax.fori_loop(0, SAMPLES, body, (jnp.zeros((16, 128), F32),) * 6)
            values = [quad_sum(t, row, lane) * (1.0 / 64.0) for t in sums]
            emit(2 * pair, values)
            emit(2 * pair + 1, values)

    far_row = core * 3
    for i, c in enumerate(RIM):
        for p in range(PLANES):
            toward[0, i, p] = part[c, p, pl.ds(far_row, 4, stride=4), :]
            toward[1, i, p] = part[c, p, pl.ds(3 - far_row, 4, stride=4), :]

    for e in range(2):
        for i in range(3):
            for p in range(PLANES):
                packed[(e * 3 + i) * PLANES + p] = toward[e, i, p]

    @pl.when(level == 0)
    def _():
        for i, c in enumerate(RIM):
            for p in range(PLANES):
                for r in (1, 2):
                    packed[23 + (i * PLANES + p) * 2 + r] = part[c, p, pl.ds(r, 4, stride=4), :]

    @pl.when(level != 0)
    def _():
        for g in range(2):
            for c in range(6):
                for pair in range(PLANES // 2):
                    packed[24 + (g * 6 + c) * 2 + pair] = part[c, 2 * pair, pl.ds(2 * g, 4, stride=4), :]


def momentum_kernel(vel, mate, far, moved, part, solvent, stored, rest, sem):
    copy = pltpu.make_async_copy(moved, stored, sem)
    copy.start()
    for i, c in enumerate(REST):
        for p in range(PLANES):
            rest[i, p] = part[c, p]
    core = lax.rem(lax.axis_index("tile"), 2)
    row, lane = row_of(), lane_of()
    velocity = [[vel[a, p] for p in range(PLANES)] for a in range(3)]
    for p in range(PLANES):
        for a in range(3):
            here = velocity[a][p]
            pairs = (
                plane_pair(velocity[a], p),
                row_pair(here, row_edges(core, mate[a, p], far[a, p]), row),
                column_pair(here, lane),
            )
            laplace = -6.0 * here
            carried = jnp.zeros_like(here)
            for b, (after, before) in enumerate(pairs):
                laplace = laplace + (after + before)
                carried = carried + velocity[b][p] * ((after - before) * 0.5)
            solvent[a, p] = here + STEP_TIME * (VISCOSITY * laplace - carried)
    copy.wait()


def stress_kernel(solvent, part, packed, rest, edges, inner, stress):
    level = lax.axis_index("lvl")
    core = lax.rem(lax.axis_index("tile"), 2)
    row, lane = row_of(), lane_of()
    far_row = core * 3

    @pl.when(level == 0)
    def _():
        for c in range(6):
            for pair in range(PLANES // 2):
                place = 24 + c * 2 + pair
                added = jnp.where(row < 2, over_runs(packed[place]), over_runs(packed[12 + place]))
                for p in (2 * pair, 2 * pair + 1):
                    stress[c, p] = part[c, p] + added

    @pl.when(level != 0)
    def _():
        for i, c in enumerate(RIM):
            for p in range(PLANES):
                stress[c, p, pl.ds(far_row, 4, stride=4), :] = edges[0, i, p]
                stress[c, p, pl.ds(3 - far_row, 4, stride=4), :] = edges[1, i, p]
                for r in (1, 2):
                    own = part[c, p, pl.ds(r, 4, stride=4), :]
                    stress[c, p, pl.ds(r, 4, stride=4), :] = own + packed[23 + (i * PLANES + p) * 2 + r]
        for i, c in enumerate(REST):
            for p in range(PLANES):
                stress[c, p] = part[c, p] + rest[i, p]

    walls = [[stress[c, p] for p in range(PLANES)] for c in (0, 3, 4)]
    for p in range(PLANES):
        for a in range(3):
            nothing = jnp.zeros((16, 128), F32)
            y_after, y_before = row_pair(stress[RIM[a], p], (nothing, nothing), row)
            x_after, x_before = plane_pair(walls[a], p)
            z_after, z_before = column_pair(stress[(4, 5, 2)[a], p], lane)
            force = (x_after - x_before) * 0.5 + (y_after - y_before) * 0.5 + (z_after - z_before) * 0.5
            inner[a, p] = solvent[a, p] + (STEP_TIME * POLYMER_WEIGHT) * force


def final_kernel(inner, from_far, from_mate, velocity_next):
    core = lax.rem(lax.axis_index("tile"), 2)
    row = row_of()
    for p in range(PLANES):
        for a in range(3):
            outer = beyond(row_edges(core, from_mate[a, p], from_far[a, p]), row)
            velocity_next[a, p] = inner[a, p] + (0.5 * STEP_TIME * POLYMER_WEIGHT) * outer


def limit(mebibytes):
    return pltpu.CompilerParams(vmem_limit_bytes=int(mebibytes * 2**20))


def shape(*extent):
    return jax.ShapeDtypeStruct(extent, F32)


def far_pairs(tiles, across):
    pairs = []
    for l in range(2):
        for t in range(1, tiles, 2):
            u = (t + 1) % tiles
            m = 1 - l if across and (t // 8) % 4 == 3 and t % 8 == 7 else l
            pairs += [(l * tiles + t, m * tiles + u), (m * tiles + u, l * tiles + t)]
    return pairs


def local(velocity, dumbbells, increments):
    tiles = lax.axis_size("tile")
    far_swap = far_pairs(tiles, False)
    rim_swap = far_pairs(tiles, True)
    mate_swap = [(t, t ^ 1) for t in range(tiles)]
    level_swap = [(0, 1), (1, 0)]
    vel = view(velocity)
    toward_far, toward_mate = pl.pallas_call(
        edge_kernel,
        out_shape=[shape(3, PLANES, 4, 128)] * 2,
        in_specs=[VMEM],
        out_specs=[VMEM] * 2,
        compiler_params=limit(2),
    )(vel)
    far = lax.ppermute(toward_far, ("lvl", "tile"), far_swap)
    mate = lax.ppermute(toward_mate, "tile", mate_swap)
    field = (3, PLANES, 16, 128)
    ensemble = (3, SAMPLES, PLANES, 16, 128)
    here, whole, first, later, slopes = pl.pallas_call(
        prepare_kernel,
        out_shape=[shape(*ensemble)] * 4 + [shape(3, 3, PLANES, 16, 128)],
        in_specs=[ANY] * 2 + [VMEM],
        out_specs=[VMEM] * 5,
        scratch_shapes=[
            pltpu.VMEM((2,) + ensemble, jnp.bfloat16),
            pltpu.SemaphoreType.DMA((SAMPLES,)),
            pltpu.SemaphoreType.DMA((SAMPLES,)),
        ],
        compiler_params=limit(50.2),
    )(view(dumbbells[0]), view(increments[0]), vel)
    moved, part, toward, packed = pl.pallas_call(
        advance_kernel,
        out_shape=[
            shape(*ensemble),
            shape(6, PLANES, 16, 128),
            shape(2, 3, PLANES, 4, 128),
            shape(48, 4, 128),
        ],
        in_specs=[VMEM] * 7,
        out_specs=[VMEM] * 4,
        compiler_params=limit(16),
    )(slopes, mate, far, here, whole, first, later)
    packed_other = lax.ppermute(packed, "lvl", level_swap)
    solvent, stored, rest = pl.pallas_call(
        momentum_kernel,
        out_shape=[shape(*field), shape(*ensemble), shape(*field)],
        in_specs=[VMEM] * 3 + [ANY, VMEM],
        out_specs=[VMEM, ANY, VMEM],
        scratch_shapes=[pltpu.SemaphoreType.DMA],
        compiler_params=limit(8),
    )(vel, mate, far, moved, part)
    rest_other = lax.ppermute(rest, "lvl", [(0, 1)])
    edges = toward + packed_other[:24].reshape(toward.shape)
    from_far = lax.ppermute(edges[0], ("lvl", "tile"), rim_swap)
    from_mate = lax.ppermute(edges[1], "tile", mate_swap)
    inner, stress = pl.pallas_call(
        stress_kernel,
        out_shape=[shape(*field), shape(6, PLANES, 16, 128)],
        in_specs=[VMEM] * 5,
        out_specs=[VMEM] * 2,
        compiler_params=limit(8),
    )(solvent, part, packed_other, rest_other, edges)
    velocity_next = pl.pallas_call(
        final_kernel,
        out_shape=shape(*field),
        in_specs=[VMEM] * 3,
        out_specs=VMEM,
        compiler_params=limit(4),
    )(inner, from_far, from_mate)
    return (unview(velocity_next), unview(stress), unview(stored)[None])


def solution(mesh):
    in_specs = (
        P(None, None, "tile", None),
        P("lvl", None, None, None, "tile", None),
        P("lvl", None, None, None, None, "tile", None),
    )
    out_specs = (
        P(None, None, "tile", None),
        P(None, None, "tile", None),
        P("lvl", None, None, None, "tile", None),
    )
    return jax.shard_map(local, mesh=mesh, in_specs=in_specs, out_specs=out_specs, check_vma=False)
```
